256 devices in a mesh: freq: 8 (over y, core), se: 32 (over z, x).
Axes of the slice: x: 4, y: 4, z: 8, core: 2. Of those that a mesh axis runs over, the one named last changes fastest.
Arguments:
- stress_modes: bfloat16 [262144, 800], P('se', 'freq'), may hold values from -6 to 6
- modal_transfer: bfloat16 [800, 48, 128], P('se', 'freq'), may hold values from -0.21875 to 0.21875
- input_psd: bfloat16 [48, 64, 128], P('freq'), as said below
- panel_super: int32 [1024, 1], replicated, may hold values from 0 to 31; in each aligned block of 32 rows (0 to 31, 32 to 63, ...) at most 2 rows name the same one
- panel_offset: int32 [1024], replicated, may hold values from 0 to 8128
- panel_count: int32 [1024], replicated, may hold values from 1 to 64, 49152 in all
Outputs:
- cross_spectra: bfloat16 [1024, 48, 64, 128], P('se', 'freq')
The draws below stay inside these ranges and needn't reach their ends.
Inputs may be any that keep to these rules, and one draw needn't show every extreme that they name: `panel_super`: among the monitored panels of each owner (the 32 consecutive entries of one block) at most 2 lie on one superelement. `input_psd`: each matrix is Hermitian positive definite.
All inputs are finite; a program needn't handle non-finite values.
Results may differ from the reference program's by a relative error of at most 0.0056.
Values may be sent and summed in bfloat16 or wider, within the bound.
A program may use at most 64 MiB of HBM per device.

```python
import math
import jax
import jax.numpy as jnp
import numpy as np
from jax import lax

MODES = 800
NI = 64
PROW = 64
PAN_DEV = 32
ROWS_DEV = 8192
FREQS = 48
PANELS = 1024
ROWS = 262144
MOST = 2
N_SE = 32


def coherent_matrices(key_real, key_imag, reach, variance, loading, scales):
    shape = (FREQS, NI, NI)
    factor_real = jax.random.randint(key_real, shape, -reach, reach + 1).astype(jnp.float32)
    factor_imag = jax.random.randint(key_imag, shape, -reach, reach + 1).astype(jnp.float32)
    exact = lax.Precision.HIGHEST
    outer_real = jnp.einsum('fck,fdk->fcd', factor_real, factor_real, precision=exact)
    outer_real = outer_real + jnp.einsum('fck,fdk->fcd', factor_imag, factor_imag, precision=exact)
    outer_imag = jnp.einsum('fck,fdk->fcd', factor_imag, factor_real, precision=exact)
    outer_imag = outer_imag - jnp.einsum('fck,fdk->fcd', factor_real, factor_imag, precision=exact)
    norming = 1.0 / (2.0 * variance * NI)
    identity = jnp.eye(NI, dtype=jnp.float32)
    both = scales[:, :, None] * scales[:, None, :]
    real_part = both * (outer_real * norming + loading * identity)
    imag_part = both * (outer_imag * norming)
    return jnp.concatenate([real_part, imag_part], axis=2)


def draw_input_psd(key, part):
    key = jax.random.fold_in(key, 7)
    key_level, key_real, key_imag = jax.random.split(key, 3)
    level = jnp.exp(jax.random.uniform(key_level, (FREQS, NI), jnp.float32, 0.0, math.log(10.0)))
    scales = jnp.sqrt(level / NI)
    spectra = coherent_matrices(key_real, key_imag, 3, 4.0, 0.25, scales)
    return spectra.astype(jnp.bfloat16)


def place_ends(array, key, smallest, largest):
    extent = array.shape
    index_at = [jax.random.randint(jax.random.fold_in(key, axis), (), 0, extent[axis]) for axis in range(len(extent))]
    array = array.at[tuple(index_at)].set(smallest)
    longest = extent.index(max(extent))
    index_at[longest] = (index_at[longest] + 1) % extent[longest]
    return array.at[tuple(index_at)].set(largest)


def steps_of(own_key, shape, pieces, smallest, high):
    factor_of = 1.0
    for position, shards_of in pieces:
        draws = jax.random.uniform(jax.random.fold_in(jax.random.fold_in(own_key, 6), position), (shards_of,), jnp.float32, smallest / len(pieces), high / len(pieces))
        factor_of = factor_of * jnp.repeat(jnp.exp(draws), shape[position] // shards_of).reshape((-1,) + (1,) * (len(shape) - 1 - position))
    return factor_of


def split_up(number_of, total, most, skew):
    loads = [(1 << 20) // math.isqrt(grade ** skew) + 1 for grade in range(2, number_of + 1)]
    rest, counts = total - most - (number_of - 1), [1] * (number_of - 1)
    while rest > 0:
        free = [i for i in range(number_of - 1) if counts[i] < most]
        whole, budget = sum([loads[i] for i in free]), rest
        for i in free:
            addition = min(most - counts[i], max(1, budget * loads[i] // whole), rest)
            counts[i] = counts[i] + addition
            rest = rest - addition
    return np.array([most] + counts)


def ragged_sizes(own_key, amount, total, limit, slope):
    if amount == 2:
        one = jax.random.randint(own_key, (), max(1, total - limit), min(limit, total - 1) + 1)
        return jnp.stack([one, total - one])
    lengths = jnp.asarray(split_up(amount, total, limit, slope), jnp.int32)
    pairs = (amount - 1) // 2
    giver, sink = lengths[1:1 + 2 * pairs:2], lengths[2:2 + 2 * pairs:2]
    room = jnp.minimum(giver - 1, limit - sink)
    moved = jax.random.randint(jax.random.fold_in(own_key, 1), (pairs,), 0, 1 << 20) % (room + 1)
    lengths = lengths.at[1:1 + 2 * pairs:2].set(giver - moved).at[2:2 + 2 * pairs:2].set(sink + moved)
    return lengths[jax.random.permutation(jax.random.fold_in(own_key, 2), amount)]


def assign_block(own_key, own, number, rows, number_of, top, most, slope):
    ranking = jax.random.permutation(own_key, number_of)
    packed, usual = portions_of(number_of, rows * top, most, slope, True), portions_of(number_of, rows * top, most, slope, False)
    places = jnp.arange(number_of)

    def named(sizes, rotation):
        used = int((sizes > 0).sum())
        fixed = max(1, used // 4)
        moved = fixed + (places - fixed + rotation * (used - fixed)) % max(1, number_of - fixed)
        return jnp.zeros((number_of,), jnp.int32).at[ranking[jnp.where(places < fixed, places, moved)]].set(jnp.asarray(sizes, jnp.int32))

    sizes = jnp.where(number % 4 == 0, named(packed, number // 4), named(usual, number - number // 4 - 1))
    mixed = jax.random.permutation(jax.random.fold_in(own, 3), number_of)
    giver, receiver = mixed[0:number_of // 2 * 2:2], mixed[1:number_of // 2 * 2:2]
    margin = jnp.minimum(sizes[giver] - 1, most - sizes[receiver]) // 2
    margin = jnp.where((giver == ranking[0]) | (receiver == ranking[0]) | (sizes[receiver] == 0), 0, jnp.maximum(margin, 0))
    moved = jax.random.randint(jax.random.fold_in(own, 4), (number_of // 2,), 0, 1 << 20) % (margin + 1)
    sizes = sizes.at[giver].add(-moved).at[receiver].add(moved)
    members = jnp.searchsorted(jnp.cumsum(sizes), jnp.arange(rows * top), side="right").astype(jnp.int32)
    listing = members.reshape(top, rows).T
    listing = listing[jax.random.permutation(jax.random.fold_in(own, 1), rows)]
    rotation = jax.random.randint(jax.random.fold_in(own, 2), (rows, 1), 0, top)
    return jnp.take_along_axis(listing, (jnp.arange(top)[None, :] + rotation) % top, axis=1)


def portions_of(amount, total, most, skew, full):
    weights = [(1 << 20) // math.isqrt(grade ** skew) + 1 for grade in range(1, amount + 1)]
    largest = most if full else min(most, max(-(-total // amount), total * weights[0] // sum(weights)))
    least = 1 if total - largest >= amount - 1 else 0
    holding, rest = [largest] + [least] * (amount - 1), total - largest - least * (amount - 1)
    while rest > 0:
        candidates = [i for i in range(1, amount) if holding[i] < largest] or [i for i in range(1, amount) if holding[i] < most]
        pool, left = sum([weights[i] for i in candidates]), rest
        for i in candidates:
            addition = min(most - holding[i], max(1, left * weights[i] // pool), rest)
            holding[i] = holding[i] + addition
            rest = rest - addition
    return np.array(holding)


def bell_draw(stream_key, shape, spread, limit, cuts=(), kind=jnp.bfloat16):
    factor_of = steps_of(stream_key, shape, cuts, -0.22, 0.18) if cuts else 1.0
    array = jax.random.normal(stream_key, shape, jnp.float32) * spread * factor_of
    return jnp.minimum(jnp.maximum(array, -limit), limit).astype(kind)


def setup_inputs(seed: int = 0) -> dict:
    seeds = jax.random.split(jax.random.key(seed), 7)
    stress_modes = bell_draw(seeds[0], (ROWS, MODES), 1.0, 6.0, ((0, 32), (1, 8)))
    modal_transfer = bell_draw(seeds[1], (MODES, FREQS, 2 * NI), MODES ** -0.5, 0.21875, ((0, 32), (1, 8)))
    input_psd = draw_input_psd(jax.random.fold_in(seeds[6], 71), 0)
    panel_super_keys = jax.random.split(jax.random.fold_in(seeds[3], 1), PANELS // PAN_DEV)
    panel_super_turns = jax.random.permutation(jax.random.fold_in(seeds[3], 3), PANELS // PAN_DEV)
    panel_super = jax.vmap(lambda own, number: assign_block(jax.random.fold_in(seeds[3], 2), own, number, PAN_DEV, N_SE, 1, MOST, 2))(panel_super_keys, panel_super_turns).reshape((PANELS, 1))
    panel_offset = place_ends(jax.random.randint(seeds[4], (PANELS,), 0, ROWS_DEV - PROW + 1), jax.random.fold_in(seeds[4], 1), 0, ROWS_DEV - PROW).astype(jnp.int32)
    panel_count = ragged_sizes(seeds[5], PANELS, PANELS * PROW * 3 // 4, PROW, 0).astype(jnp.int32)
    return dict(stress_modes=stress_modes, modal_transfer=modal_transfer, input_psd=input_psd, panel_super=panel_super, panel_offset=panel_offset, panel_count=panel_count)


def build_block(input_psd):
    real_part = input_psd[:, :, :NI]
    imag_part = input_psd[:, :, NI:]
    upper = jnp.concatenate([real_part, imag_part], axis=2)
    lower = jnp.concatenate([-imag_part, real_part], axis=2)
    return jnp.concatenate([upper, lower], axis=1)


def reference(stress_modes, modal_transfer, input_psd, panel_super, panel_offset, panel_count):
    flat = modal_transfer.reshape(MODES, FREQS * 2 * NI)
    block = build_block(input_psd).astype(jnp.float32)
    zero = jnp.zeros((), jnp.bfloat16)

    def one_panel(index):
        start = (panel_super[index, 0] * ROWS_DEV + panel_offset[index]).astype(jnp.int32)
        rows = lax.dynamic_slice_in_dim(stress_modes, start, PROW, 0)
        response = jnp.dot(rows, flat, preferred_element_type=jnp.float32).astype(jnp.bfloat16)
        live = jnp.arange(PROW, dtype=jnp.int32) < panel_count[index]
        response = jnp.where(live[:, None], response, zero).reshape(PROW, FREQS, 2 * NI)
        wide = response.astype(jnp.float32)
        mixed = jnp.einsum("rfc,fcd->rfd", wide, block).astype(jnp.bfloat16)
        turned = jnp.concatenate([mixed[..., NI:], -mixed[..., :NI]], axis=2)
        cross_real = jnp.einsum("ifc,jfc->fij", mixed.astype(jnp.float32), wide)
        cross_imag = jnp.einsum("ifc,jfc->fij", turned.astype(jnp.float32), wide)
        return jnp.concatenate([cross_real, cross_imag], axis=2).astype(jnp.bfloat16)

    return lax.map(one_panel, jnp.arange(PANELS, dtype=jnp.int32))
```

```python
import functools

import jax
import jax.numpy as jnp
from jax import lax
from jax.experimental import pallas as pl
from jax.experimental.pallas import tpu as pltpu
from jax.sharding import PartitionSpec as P

MESH = pl.DeviceIdType.MESH
MODES = 800
NI = 64
PROW = 64
FREQ_DEV = 6
PAN_DEV = 32
NF = 8
NZ = 8
NX = 4
NS = NZ * NX
LOCAL = MODES // NF
SHARD = MODES // NS
CHUNKS = ((0, 48), (48, 32), (80, 32))
PADDED = 112
LANES = PAN_DEV * PROW
WIDE = FREQ_DEV * 2 * NI
TSH = 32
f32 = jnp.float32
bf16 = jnp.bfloat16


def div(a, b):
    return lax.div(a, jnp.int32(b))


def rem(a, b):
    return lax.rem(a, jnp.int32(b))


def response_kernel(
    sup_hbm, off_hbm, cnt_hbm, table_hbm, t_hbm, psd_hbm, resp_ref, blocks_ref,
    sup, off, cnt, t_ref, psd_ref, in_sem, table, send_buf, rb0, rb1, rb2, xb0, xb1, xb2, tbuf, tin, acc, tt, perm,
    ranks, table_sem, a2a_send, a2a_recv, y_send, y_recv, tz_send, tz_recv, tx_send, tx_recv,
):
    rbs, xbs = (rb0, rb1, rb2), (xb0, xb1, xb2)
    f = lax.axis_index("freq")
    me = lax.axis_index("se")
    z, x = div(me, NX), rem(me, NX)
    up, down = rem(f + 2, NF), rem(f + NF - 2, NF)
    across = rem(f + 4, NF)
    twin = f + 1 - 2 * rem(f, 2)
    x_up = z * NX + rem(x + 1, NX)
    x_down = z * NX + rem(x + NX - 1, NX)

    small = [
        pltpu.make_async_copy(source, to, in_sem.at[k])
        for k, (source, to) in enumerate(
            ((t_hbm, t_ref), (sup_hbm, sup), (off_hbm, off), (cnt_hbm, cnt), (psd_hbm, psd_ref))
        )
    ]
    for copy in small:
        copy.start()
    tiles = table.shape[0]

    @pl.loop(0, tiles)
    def _(t):
        part = table_hbm.at[:, pl.ds(pl.multiple_of(t * 128, 128), 128)]
        pltpu.make_async_copy(part, table.at[t], table_sem).start()

    barrier = pltpu.get_barrier_semaphore()

    @pl.loop(1, NS)
    def _(i):
        pl.semaphore_signal(barrier, 1, device_id={"se": rem(me + i, NS)}, device_id_type=MESH)

    for g in (up, down, twin):
        pl.semaphore_signal(barrier, 1, device_id={"freq": g}, device_id_type=MESH)

    tin[...] = jnp.zeros_like(tin)
    small[0].wait()
    tin[:, 0:SHARD, :] = t_ref[...]
    tbuf[x, z] = tin[...]
    send_buf[:, PADDED - 16 : PADDED, :] = jnp.zeros((NS, 16, 128), bf16)

    pl.semaphore_wait(barrier, NS - 1 + 3)

    def tz_copy(i):
        return pltpu.make_async_remote_copy(
            src_ref=tbuf.at[x, z], dst_ref=tbuf.at[x, z], send_sem=tz_send, recv_sem=tz_recv,
            device_id={"se": rem(z + i, NZ) * NX + x}, device_id_type=MESH,
        )

    @pl.loop(1, NZ)
    def _(i):
        tz_copy(i).start()

    small[1].wait()
    small[2].wait()
    pltpu.make_async_copy(table, table, table_sem).wait()

    lane = lax.broadcasted_iota(jnp.int32, (LOCAL, 128), 1)

    def window(start, place):
        tile = div(start, 128)
        inside = start - tile * 128
        a = table[tile].astype(f32)
        b = table[jnp.minimum(tile + 1, tiles - 1)].astype(f32)
        both = jnp.where(lane >= inside, a, b)
        return pltpu.roll(both, rem(place + 128 - inside, 128), 1)

    def gather(o):
        base = o * PAN_DEV
        first, last = jnp.int32(0), jnp.int32(0)
        hits = [sup[base + j] == me for j in range(PAN_DEV)]
        starts = [off[base + j] for j in range(PAN_DEV)]
        for j in range(PAN_DEV):
            last = jnp.where(hits[j], starts[j], last)
            k = PAN_DEV - 1 - j
            first = jnp.where(hits[k], starts[k], first)
        got = jnp.where(lane < PROW, window(first, 0), window(last, PROW)).astype(bf16)
        send_buf[o, 0:LOCAL, :] = got

    def a2a_copy(c, o):
        r0, rows = CHUNKS[c]
        return pltpu.make_async_remote_copy(
            src_ref=send_buf.at[o, pl.ds(r0, rows)], dst_ref=rbs[c].at[me],
            send_sem=a2a_send.at[c], recv_sem=a2a_recv.at[c],
            device_id={"se": o}, device_id_type=MESH,
        )

    @pl.loop(1, NS)
    def _(i):
        o = rem(me + i, NS)
        gather(o)
        a2a_copy(0, o).start()

    for c in range(1, len(CHUNKS)):

        @pl.loop(1, NS)
        def _(i):
            a2a_copy(c, rem(me + i, NS)).start()

    gather(me)
    for c, (r0, rows) in enumerate(CHUNKS):
        rbs[c][me] = send_buf[me, r0 : r0 + rows, :]

    def tz_all():
        return pltpu.make_async_copy(tbuf.at[0, 0 : NZ - 1], tbuf.at[0, 0 : NZ - 1], tz_recv)

    def tx_copy(k):
        if k < 2:
            source, to = tbuf.at[x], (x_up, x_down)[k]
        elif k == 2:
            source, to = tbuf.at[rem(x + NX - 1, NX), 0 : NZ // 2], x_up
        else:
            source, to = tbuf.at[rem(x + 1, NX), NZ // 2 : NZ], x_down
        return pltpu.make_async_remote_copy(
            src_ref=source, dst_ref=source, send_sem=tx_send.at[k], recv_sem=tx_recv.at[k],
            device_id={"se": to}, device_id_type=MESH,
        )

    tz_all().wait()
    tx_copy(0).start()
    tx_copy(1).start()

    small[3].wait()
    small[4].wait()
    half_lane = lax.broadcasted_iota(jnp.int32, (NI, 128), 1)
    for g in range(FREQ_DEV):
        turned = pltpu.roll(psd_ref[g].astype(f32), NI, 1)
        blocks_ref[g, 0:NI, :] = psd_ref[g]
        blocks_ref[g, NI:128, :] = jnp.where(half_lane < NI, -turned, turned).astype(bf16)

    mine = me * PAN_DEV
    own = [sup[mine + p] for p in range(PAN_DEV)]
    for p in range(PAN_DEV):
        rank = jnp.int32(0)
        for e in range(p):
            rank = jnp.where(own[e] == own[p], 1, rank)
        ranks[p] = rank

    row = lax.broadcasted_iota(jnp.int32, (128, 1), 0)
    column = lax.broadcasted_iota(jnp.int32, (128, PADDED * NF), 1)

    @pl.loop(0, NS * TSH // 128)
    def _(b):
        at = row + b * 128
        shard = div(at, TSH)
        place = rem(at, TSH)
        of_z, of_x = rem(shard, NZ), div(shard, NZ)
        mode = of_x * SHARD + place
        target = jnp.full((128, 1), -1, jnp.int32)
        for r0, rows in CHUNKS:
            inside = (mode >= r0) & (mode < r0 + rows)
            target = jnp.where(inside, r0 * NF + of_z * rows + mode - r0, target)
        target = jnp.where(place < SHARD, target, -1)
        perm[pl.ds(pl.multiple_of(b * 128, 128), 128), :] = jnp.where(column == target, 1.0, 0.0).astype(bf16)

    def select(c):
        rows = CHUNKS[c][1]
        all_c = rbs[c].at[0 : NS - 1]
        pltpu.make_async_copy(all_c, all_c, a2a_recv.at[c]).wait()
        at = lax.broadcasted_iota(jnp.int32, (rows, 128), 1)

        @pl.loop(0, PAN_DEV // 2)
        def _(q):
            p = 2 * q
            left = rbs[c][sup[mine + p]].astype(f32)
            right = rbs[c][sup[mine + p + 1]].astype(f32)
            left = pltpu.roll(left, PROW * ranks[p], 1)
            right = pltpu.roll(right, PROW * (1 - ranks[p + 1]), 1)
            live = jnp.where(at < PROW, cnt[mine + p], cnt[mine + p + 1] + PROW)
            pair = jnp.where(at < live, jnp.where(at < PROW, left, right), 0.0)
            xbs[c][f, :, pl.ds(pl.multiple_of(q * 128, 128), 128)] = pair.astype(bf16)

    def y_copy(c, k):
        xb = xbs[c]
        half = LANES // 2
        source, to = (
            (xb.at[f], up),
            (xb.at[f], down),
            (xb.at[down, :, 0:half], up),
            (xb.at[up, :, half:LANES], down),
            (xb.at[f], twin),
            (xb.at[down], twin),
            (xb.at[up], twin),
            (xb.at[across], twin),
        )[k]
        return pltpu.make_async_remote_copy(
            src_ref=source, dst_ref=source, send_sem=y_send.at[c, k], recv_sem=y_recv.at[c, k],
            device_id={"freq": to}, device_id_type=MESH,
        )

    def y_begin(c):
        for k in (0, 1, 4):
            y_copy(c, k).start()

    def y_forward(c):
        y_copy(c, 0).wait_recv()
        y_copy(c, 2).start()
        y_copy(c, 5).start()
        y_copy(c, 1).wait_recv()
        y_copy(c, 3).start()
        y_copy(c, 6).start()

    def y_last(c):
        y_copy(c, 2).wait_recv()
        y_copy(c, 3).wait_recv()
        y_copy(c, 7).start()

    def y_end(c):
        for k in (4, 5, 6, 7):
            y_copy(c, k).wait_recv()

    def multiply(c):
        r0, rows = CHUNKS[c]
        deep = rows * NF
        step = 256

        @pl.loop(0, LANES // step)
        def _(n):
            at = pl.ds(pl.multiple_of(n * step, step), step)
            block = xbs[c][:, :, at].reshape(deep, step)
            part = jnp.dot(tt[:, r0 * NF : r0 * NF + deep], block, preferred_element_type=f32)
            if c > 0:
                part = part + acc[:, at]
            if c < len(CHUNKS) - 1:
                acc[:, at] = part
            else:
                resp_ref[:, at] = part.astype(bf16)

    select(0)
    y_begin(0)
    tx_copy(0).wait_recv()
    tx_copy(2).start()
    tx_copy(1).wait_recv()
    tx_copy(3).start()
    y_forward(0)
    tx_copy(2).wait_recv()
    tx_copy(3).wait_recv()
    for g in range(FREQ_DEV):
        block = tbuf[:, :, g].reshape(NS * TSH, 128)
        tt[g * 128 : (g + 1) * 128, :] = lax.dot_general(
            block, perm[...], (((0,), (0,)), ((), ())), preferred_element_type=f32
        ).astype(bf16)
    y_last(0)
    select(1)
    y_begin(1)
    y_end(0)
    multiply(0)
    y_forward(1)
    y_last(1)
    select(2)
    y_begin(2)
    y_end(1)
    multiply(1)
    y_forward(2)
    y_last(2)
    y_end(2)
    multiply(2)

    sent = tbuf.at[0, 0 : NZ - 1]
    pltpu.make_async_copy(sent, sent, tz_send).wait()
    for k in range(4):
        tx_copy(k).wait_send()
    for c in range(len(CHUNKS)):
        sent = rbs[c].at[0 : NS - 1]
        pltpu.make_async_copy(sent, sent, a2a_send.at[c]).wait()
        for k in range(8):
            y_copy(c, k).wait_send()


def responses(sup, off, cnt, table, transfer, psd):
    return pl.pallas_call(
        response_kernel,
        out_shape=[
            jax.ShapeDtypeStruct((WIDE, LANES), bf16),
            jax.ShapeDtypeStruct((FREQ_DEV, 128, 128), bf16),
        ],
        in_specs=[pl.BlockSpec(memory_space=pltpu.HBM)] * 6,
        out_specs=[pl.BlockSpec(memory_space=pltpu.VMEM)] * 2,
        scratch_shapes=[
            *[pltpu.SMEM(a.shape, jnp.int32) for a in (sup, off, cnt)],
            pltpu.VMEM(transfer.shape, bf16),
            pltpu.VMEM(psd.shape, bf16),
            pltpu.SemaphoreType.DMA((5,)),
            pltpu.VMEM((table.shape[1] // 128, LOCAL, 128), bf16),
            pltpu.VMEM((NS, PADDED, 128), bf16),
            *[pltpu.VMEM((NS, rows, 128), bf16) for _, rows in CHUNKS],
            *[pltpu.VMEM((NF, rows, LANES), bf16) for _, rows in CHUNKS],
            pltpu.VMEM((NX, NZ, FREQ_DEV, TSH, 128), bf16),
            pltpu.VMEM((FREQ_DEV, TSH, 128), bf16),
            pltpu.VMEM((WIDE, LANES), f32),
            pltpu.VMEM((WIDE, PADDED * NF), bf16),
            pltpu.VMEM((NS * TSH, PADDED * NF), bf16),
            pltpu.SMEM((PAN_DEV,), jnp.int32),
            pltpu.SemaphoreType.DMA,
            pltpu.SemaphoreType.DMA((len(CHUNKS),)),
            pltpu.SemaphoreType.DMA((len(CHUNKS),)),
            pltpu.SemaphoreType.DMA((len(CHUNKS), 8)),
            pltpu.SemaphoreType.DMA((len(CHUNKS), 8)),
            pltpu.SemaphoreType.DMA,
            pltpu.SemaphoreType.DMA,
            pltpu.SemaphoreType.DMA((4,)),
            pltpu.SemaphoreType.DMA((4,)),
        ],
        compiler_params=pltpu.CompilerParams(
            collective_id=0, has_side_effects=True, vmem_limit_bytes=44 * 2**20
        ),
        name="responses",
    )(*[pltpu.with_memory_space_constraint(a, pltpu.HBM) for a in (sup, off, cnt, table, transfer, psd)])


def spectra_kernel(resp_ref, blocks, out_ref):
    lane = lax.broadcasted_iota(jnp.int32, (NI, 128), 1)

    for g in range(FREQ_DEV):
        for h in range(2):
            resp = resp_ref[g * 128 : (g + 1) * 128, h * 128 : (h + 1) * 128]
            mixed = lax.dot_general(
                resp, blocks[g], (((0,), (0,)), ((), ())), preferred_element_type=f32
            ).astype(bf16)
            turned = jnp.concatenate([-resp[NI:], resp[:NI]], axis=0)
            both = jnp.concatenate([resp, turned], axis=1)
            cross = jnp.dot(mixed, both, preferred_element_type=f32)
            real, imag = cross[:, 0:128], cross[:, 128:256]
            out_ref[2 * h, g] = jnp.where(lane < NI, real[0:NI], pltpu.roll(imag[0:NI], NI, 1)).astype(bf16)
            out_ref[2 * h + 1, g] = jnp.where(lane < NI, pltpu.roll(real[NI:], NI, 1), imag[NI:]).astype(bf16)


def spectra(resp, blocks):
    step = 256
    return pl.pallas_call(
        spectra_kernel,
        grid=(LANES // step,),
        out_shape=jax.ShapeDtypeStruct((PAN_DEV, FREQ_DEV, PROW, 2 * NI), bf16),
        in_specs=[
            pl.BlockSpec((WIDE, step), lambda i: (0, i)),
            pl.BlockSpec((FREQ_DEV, 128, 128), lambda i: (0, 0, 0)),
        ],
        out_specs=pl.BlockSpec((step // PROW, FREQ_DEV, PROW, 2 * NI), lambda i: (i, 0, 0, 0)),
        name="spectra",
    )(resp, blocks)


def per_device(stress_modes, modal_transfer, input_psd, panel_super, panel_offset, panel_count):
    resp, blocks = responses(
        panel_super.reshape(-1), panel_offset, panel_count,
        stress_modes.T, modal_transfer.transpose(1, 0, 2), input_psd,
    )
    return spectra(resp, blocks)


def solution(mesh):
    in_specs = (P("se", "freq"), P("se", "freq", None), P("freq", None, None), P(), P(), P())
    out_specs = P("se", "freq", None, None)
    return jax.shard_map(
        per_device, mesh=mesh, in_specs=in_specs, out_specs=out_specs, check_vma=False
    )
```

```python
import functools

import jax
import jax.numpy as jnp
from jax import lax
from jax.experimental import pallas as pl
from jax.experimental.pallas import tpu as pltpu
from jax.sharding import PartitionSpec as P

MESH = pl.DeviceIdType.MESH
MODES = 800
NI = 64
PROW = 64
FREQ_DEV = 6
PAN_DEV = 32
NF = 8
NZ = 8
NX = 4
NS = NZ * NX
LOCAL = MODES // NF
SHARD = MODES // NS
CHUNKS = ((0, 32), (32, 32), (64, 32), (96, 16))
PLACES = ((0, 0), (0, 256), (1, 0), (1, 256))
DEEP = (512, 384)
PADDED = 112
LANES = PAN_DEV * PROW
WIDE = FREQ_DEV * 2 * NI
TSH = 32
f32 = jnp.float32
bf16 = jnp.bfloat16


def div(a, b):
    return lax.div(a, jnp.int32(b))


def rem(a, b):
    return lax.rem(a, jnp.int32(b))


def response_kernel(
    sup_hbm, off_hbm, cnt_hbm, table_hbm, t_hbm, psd_hbm, resp_ref, blocks_ref,
    sup, off, cnt, t_ref, psd_ref, in_sem, table, send_buf, rb0, rb1, rb2, rb3, xg0, xg1, tg0, tg1,
    tbuf, tin, acc, ranks,
    table_sem, a2a_send, a2a_recv, y_send, y_recv, tz_send, tz_recv, tx_send, tx_recv,
):
    rbs, xgs, tgs = (rb0, rb1, rb2, rb3), (xg0, xg1), (tg0, tg1)
    f = lax.axis_index("freq")
    me = lax.axis_index("se")
    z, x = div(me, NX), rem(me, NX)
    up, down = rem(f + 2, NF), rem(f + NF - 2, NF)
    across = rem(f + 4, NF)
    twin = f + 1 - 2 * rem(f, 2)
    x_up, x_down = rem(x + 1, NX), rem(x + NX - 1, NX)

    barrier = pltpu.get_barrier_semaphore()

    @pl.loop(1, NS)
    def _(i):
        pl.semaphore_signal(barrier, 1, device_id={"se": rem(me + i, NS)}, device_id_type=MESH)

    for g in (up, down, across, twin):
        pl.semaphore_signal(barrier, 1, device_id={"freq": g}, device_id_type=MESH)

    small = [
        pltpu.make_async_copy(source, to, in_sem.at[k])
        for k, (source, to) in enumerate(
            ((t_hbm, t_ref), (sup_hbm, sup), (off_hbm, off), (cnt_hbm, cnt), (psd_hbm, psd_ref))
        )
    ]
    for copy in small:
        copy.start()
    tiles = table.shape[0]

    @pl.loop(0, tiles)
    def _(t):
        part = table_hbm.at[:, pl.ds(pl.multiple_of(t * 128, 128), 128)]
        pltpu.make_async_copy(part, table.at[t], table_sem).start()

    tin[...] = jnp.zeros_like(tin)
    small[0].wait()
    tin[:, 0:SHARD, :] = t_ref[...]
    tbuf[x, z] = tin[...]
    send_buf[:, PADDED - 16 : PADDED, :] = jnp.zeros((NS, 16, 128), bf16)

    pl.semaphore_wait(barrier, NS - 1 + 4)

    def tz_at(d):
        return rem(z + NZ + d, NZ)

    def tz_copy(step, k):
        half = FREQ_DEV // 2
        if step == 0:
            source, d = tbuf.at[x, z], (1, -1, 2, -2)[k]
        else:
            source, d = (
                (tbuf.at[x, tz_at(-2)], 1),
                (tbuf.at[x, tz_at(2)], -1),
                (tbuf.at[x, tz_at(-2), 0:half], 2),
                (tbuf.at[x, tz_at(2), half:FREQ_DEV], -2),
            )[k]
        return pltpu.make_async_remote_copy(
            src_ref=source, dst_ref=source, send_sem=tz_send.at[step], recv_sem=tz_recv.at[step],
            device_id={"se": tz_at(d) * NX + x}, device_id_type=MESH,
        )

    def tz_start(step):
        for k in range(4):
            tz_copy(step, k).start()

    def tz_wait(semaphores, step):
        some = tbuf.at[0, 0 : 4 - step]
        pltpu.make_async_copy(some, some, semaphores.at[step]).wait()

    tz_start(0)

    lane = lax.broadcasted_iota(jnp.int32, (LOCAL, 128), 1)

    def window(start, place):
        tile = div(start, 128)
        inside = start - tile * 128
        a = table[tile].astype(f32)
        b = table[jnp.minimum(tile + 1, tiles - 1)].astype(f32)
        both = jnp.where(lane >= inside, a, b)
        return pltpu.roll(both, rem(place + 128 - inside, 128), 1)

    def gather(o):
        base = o * PAN_DEV
        first, last = jnp.int32(0), jnp.int32(0)
        hits = [sup[base + j] == me for j in range(PAN_DEV)]
        starts = [off[base + j] for j in range(PAN_DEV)]
        for j in range(PAN_DEV):
            last = jnp.where(hits[j], starts[j], last)
            k = PAN_DEV - 1 - j
            first = jnp.where(hits[k], starts[k], first)
        got = jnp.where(lane < PROW, window(first, 0), window(last, PROW)).astype(bf16)
        send_buf[o, 0:LOCAL, :] = got

    def a2a_copy(c, o):
        r0, rows = CHUNKS[c]
        return pltpu.make_async_remote_copy(
            src_ref=send_buf.at[o, pl.ds(r0, rows)], dst_ref=rbs[c].at[me],
            send_sem=a2a_send.at[c], recv_sem=a2a_recv.at[c],
            device_id={"se": o}, device_id_type=MESH,
        )

    def a2a_start(c):
        @pl.loop(1, NS)
        def _(i):
            a2a_copy(c, rem(me + i, NS)).start()

    def a2a_sent(c):
        sent = rbs[c].at[0 : NS - 1]
        pltpu.make_async_copy(sent, sent, a2a_send.at[c]).wait()

    small[1].wait()
    small[2].wait()
    pltpu.make_async_copy(table, table, table_sem).wait()
    @pl.loop(0, NS, unroll=4)
    def _(o):
        gather(o)

    tz_wait(tz_recv, 0)
    tz_start(1)
    for c in range(len(CHUNKS)):
        a2a_start(c)
    for c, (r0, rows) in enumerate(CHUNKS):
        rbs[c][me] = send_buf[me, r0 : r0 + rows, :]

    def tx_copy(k):
        half = NZ // 2
        source, to = (
            (tbuf.at[x, 0:half], x_up),
            (tbuf.at[x, half:NZ], x_down),
            (tbuf.at[x, half:NZ], x_up),
            (tbuf.at[x, 0:half], x_down),
            (tbuf.at[x_down, 0:half], x_up),
            (tbuf.at[x_up, half:NZ], x_down),
        )[k]
        return pltpu.make_async_remote_copy(
            src_ref=source, dst_ref=source, send_sem=tx_send.at[k], recv_sem=tx_recv.at[k],
            device_id={"se": z * NX + to}, device_id_type=MESH,
        )

    tz_wait(tz_recv, 1)
    for k in range(4):
        tx_copy(k).start()

    small[3].wait()
    small[4].wait()
    half_lane = lax.broadcasted_iota(jnp.int32, (NI, 128), 1)
    i = lax.broadcasted_iota(jnp.int32, (128, 128), 0)
    j = lax.broadcasted_iota(jnp.int32, (128, 128), 1)
    swap = jnp.where(j == i + NI, 1.0, jnp.where(i == j + NI, -1.0, 0.0)).astype(bf16)
    for g in range(FREQ_DEV):
        turned = pltpu.roll(psd_ref[g].astype(f32), NI, 1)
        blocks_ref[g, 0:NI, 0:128] = psd_ref[g]
        blocks_ref[g, NI:128, 0:128] = jnp.where(half_lane < NI, -turned, turned).astype(bf16)
        blocks_ref[g, :, 128:256] = swap

    mine = me * PAN_DEV
    own = [sup[mine + p] for p in range(PAN_DEV)]
    for p in range(PAN_DEV):
        rank = jnp.int32(0)
        for e in range(p):
            rank = jnp.where(own[e] == own[p], 1, rank)
        ranks[p] = rank

    def rows_at(c, slot):
        rows = CHUNKS[c][1]
        return pl.ds(pl.multiple_of(PLACES[c][1] + slot * rows, 16), rows)

    def select(c):
        rows = CHUNKS[c][1]
        all_c = rbs[c].at[0 : NS - 1]
        pltpu.make_async_copy(all_c, all_c, a2a_recv.at[c]).wait()
        at = lax.broadcasted_iota(jnp.int32, (rows, 128), 1)

        @pl.loop(0, PAN_DEV // 2, unroll=4)
        def _(q):
            p = 2 * q
            left = rbs[c][sup[mine + p]].astype(f32)
            right = rbs[c][sup[mine + p + 1]].astype(f32)
            left = pltpu.roll(left, PROW * ranks[p], 1)
            right = pltpu.roll(right, PROW * (1 - ranks[p + 1]), 1)
            live = jnp.where(at < PROW, cnt[mine + p], cnt[mine + p + 1] + PROW)
            pair = jnp.where(at < live, jnp.where(at < PROW, left, right), 0.0)
            xgs[PLACES[c][0]][rows_at(c, f), pl.ds(pl.multiple_of(q * 128, 128), 128)] = pair.astype(bf16)

    def y_copy(c, k):
        slot, to = ((f, up), (f, down), (f, across), (f, twin), (down, twin), (up, twin), (across, twin))[k]
        source = xgs[PLACES[c][0]].at[rows_at(c, slot)]
        return pltpu.make_async_remote_copy(
            src_ref=source, dst_ref=source, send_sem=y_send.at[c, k], recv_sem=y_recv.at[c, k],
            device_id={"freq": to}, device_id_type=MESH,
        )

    def y_begin(c):
        for k in range(4):
            y_copy(c, k).start()

    def y_relay(c):
        for k in range(3):
            y_copy(c, k).wait_recv()
            y_copy(c, k + 4).start()

    def y_end(c):
        for k in range(3, 7):
            y_copy(c, k).wait_recv()

    def tx_forward():
        for k in (0, 1):
            tx_copy(k).wait_recv()
            tx_copy(k + 4).start()

    def tx_end():
        for k in (2, 3, 4, 5):
            tx_copy(k).wait_recv()

    def compact():
        k = lax.broadcasted_iota(jnp.int32, (PADDED, 128), 0)
        at = lax.broadcasted_iota(jnp.int32, (PADDED, 128), 1)
        mode = jnp.where(rem(at, TSH) < SHARD, div(at, TSH) * SHARD + rem(at, TSH), -1)
        pick = jnp.where(k == mode, 1.0, 0.0).astype(bf16)

        @pl.loop(0, NZ)
        def _(zz):
            blocks = [tbuf[:, zz, g].reshape(NX * TSH, 128) for g in range(FREQ_DEV)]
            rows_of = jnp.dot(pick, jnp.concatenate(blocks, axis=1), preferred_element_type=f32).astype(bf16)
            for c, (r0, rows) in enumerate(CHUNKS):
                tgs[PLACES[c][0]][rows_at(c, zz), :] = rows_of[r0 : r0 + rows]

    def multiply(group):
        step = 512

        @pl.loop(0, LANES // step)
        def _(n):
            at = pl.ds(pl.multiple_of(n * step, step), step)
            part = lax.dot_general(
                xgs[group][:, at], tgs[group][...], (((0,), (0,)), ((), ())), preferred_element_type=f32
            )
            if group == 0:
                acc[at, :] = part
            else:
                resp_ref[at, :] = (acc[at, :] + part).astype(bf16)

    select(0)
    y_begin(0)
    tx_forward()
    select(1)
    y_begin(1)
    y_relay(0)
    select(2)
    y_begin(2)
    tx_end()
    compact()
    y_relay(1)
    select(3)
    y_begin(3)
    y_end(0)
    y_end(1)
    multiply(0)
    y_relay(2)
    y_relay(3)
    y_end(2)
    y_end(3)
    multiply(1)

    tz_wait(tz_send, 0)
    tz_wait(tz_send, 1)
    for c in range(len(CHUNKS)):
        a2a_sent(c)
    for k in range(6):
        tx_copy(k).wait_send()
    for c in range(len(CHUNKS)):
        for k in range(7):
            y_copy(c, k).wait_send()


def responses(sup, off, cnt, table, transfer, psd):
    return pl.pallas_call(
        response_kernel,
        out_shape=[
            jax.ShapeDtypeStruct((LANES, WIDE), bf16),
            jax.ShapeDtypeStruct((FREQ_DEV, 128, 256), bf16),
        ],
        in_specs=[pl.BlockSpec(memory_space=pltpu.HBM)] * 6,
        out_specs=[pl.BlockSpec(memory_space=pltpu.VMEM)] * 2,
        scratch_shapes=[
            *[pltpu.SMEM(a.shape, jnp.int32) for a in (sup, off, cnt)],
            pltpu.VMEM(transfer.shape, bf16),
            pltpu.VMEM(psd.shape, bf16),
            pltpu.SemaphoreType.DMA((5,)),
            pltpu.VMEM((table.shape[1] // 128, LOCAL, 128), bf16),
            pltpu.VMEM((NS, PADDED, 128), bf16),
            *[pltpu.VMEM((NS, rows, 128), bf16) for _, rows in CHUNKS],
            *[pltpu.VMEM((deep, LANES), bf16) for deep in DEEP],
            *[pltpu.VMEM((deep, WIDE), bf16) for deep in DEEP],
            pltpu.VMEM((NX, NZ, FREQ_DEV, TSH, 128), bf16),
            pltpu.VMEM((FREQ_DEV, TSH, 128), bf16),
            pltpu.VMEM((LANES, WIDE), f32),
            pltpu.SMEM((PAN_DEV,), jnp.int32),
            pltpu.SemaphoreType.DMA,
            pltpu.SemaphoreType.DMA((len(CHUNKS),)),
            pltpu.SemaphoreType.DMA((len(CHUNKS),)),
            pltpu.SemaphoreType.DMA((len(CHUNKS), 7)),
            pltpu.SemaphoreType.DMA((len(CHUNKS), 7)),
            pltpu.SemaphoreType.DMA((2,)),
            pltpu.SemaphoreType.DMA((2,)),
            pltpu.SemaphoreType.DMA((6,)),
            pltpu.SemaphoreType.DMA((6,)),
        ],
        compiler_params=pltpu.CompilerParams(
            collective_id=0, has_side_effects=True, vmem_limit_bytes=44 * 2**20
        ),
        name="responses",
    )(*[pltpu.with_memory_space_constraint(a, pltpu.HBM) for a in (sup, off, cnt, table, transfer, psd)])


def spectra_kernel(resp_ref, blocks_ref, out_ref):
    for g in range(FREQ_DEV):
        resp = resp_ref[:, g * 128 : (g + 1) * 128]
        both = jnp.dot(resp, blocks_ref[g], preferred_element_type=f32).astype(bf16)
        for h in range(0, out_ref.shape[0], 2):
            one = slice(h * PROW, (h + 1) * PROW)
            two = slice((h + 1) * PROW, (h + 2) * PROW)
            pair = slice(h * PROW, (h + 2) * PROW)
            other = jnp.concatenate([resp[one], both[one, 128:256], resp[two], both[two, 128:256]], axis=0)
            cross = lax.dot_general(
                both[pair, 0:128], other, (((1,), (1,)), ((), ())), preferred_element_type=f32
            )
            out_ref[h, g] = cross[0:PROW, 0:128].astype(bf16)
            out_ref[h + 1, g] = cross[PROW:, 128:256].astype(bf16)


def spectra(resp, blocks):
    step = 512
    return pl.pallas_call(
        spectra_kernel,
        grid=(LANES // step,),
        out_shape=jax.ShapeDtypeStruct((PAN_DEV, FREQ_DEV, PROW, 2 * NI), bf16),
        in_specs=[
            pl.BlockSpec((step, WIDE), lambda i: (i, 0)),
            pl.BlockSpec((FREQ_DEV, 128, 256), lambda i: (0, 0, 0)),
        ],
        out_specs=pl.BlockSpec((step // PROW, FREQ_DEV, PROW, 2 * NI), lambda i: (i, 0, 0, 0)),
        compiler_params=pltpu.CompilerParams(vmem_limit_bytes=16 * 2**20),
        name="spectra",
    )(resp, blocks)


def per_device(stress_modes, modal_transfer, input_psd, panel_super, panel_offset, panel_count):
    resp, blocks = responses(
        panel_super.reshape(-1), panel_offset, panel_count,
        stress_modes.T, modal_transfer.transpose(1, 0, 2), input_psd,
    )
    return spectra(resp, blocks)


def solution(mesh):
    in_specs = (P("se", "freq"), P("se", "freq", None), P("freq", None, None), P(), P(), P())
    out_specs = P("se", "freq", None, None)
    return jax.shard_map(
        per_device, mesh=mesh, in_specs=in_specs, out_specs=out_specs, check_vma=False
    )
```

```python
import functools

import jax
import jax.numpy as jnp
from jax import lax
from jax.experimental import pallas as pl
from jax.experimental.pallas import tpu as pltpu
from jax.sharding import PartitionSpec as P

MESH = pl.DeviceIdType.MESH
MODES = 800
NI = 64
PROW = 64
FREQ_DEV = 6
PAN_DEV = 32
NF = 8
NZ = 8
NX = 4
NS = NZ * NX
LOCAL = MODES // NF
SHARD = MODES // NS
CHUNKS = ((0, 32), (32, 32), (64, 32), (96, 16))
PLACES = ((0, 0), (0, 256), (1, 0), (1, 256))
DEEP = (512, 384)
PADDED = 112
LANES = PAN_DEV * PROW
WIDE = FREQ_DEV * 2 * NI
TSH = 32
f32 = jnp.float32
bf16 = jnp.bfloat16


def div(a, b):
    return lax.div(a, jnp.int32(b))


def rem(a, b):
    return lax.rem(a, jnp.int32(b))


def response_kernel(
    sup_hbm, off_hbm, cnt_hbm, table_hbm, t_hbm, psd_hbm, resp_ref, blocks_ref,
    sup, off, cnt, t_ref, psd_ref, in_sem, table, send_buf, rb0, rb1, rb2, rb3, xg0, xg1, tg0, tg1,
    tbuf, tin, acc, ranks,
    table_sem, a2a_send, a2a_recv, y_send, y_recv, tz_send, tz_recv, tx_send, tx_recv,
):
    rbs, xgs, tgs = (rb0, rb1, rb2, rb3), (xg0, xg1), (tg0, tg1)
    f = lax.axis_index("freq")
    me = lax.axis_index("se")
    z, x = div(me, NX), rem(me, NX)
    up, down = rem(f + 2, NF), rem(f + NF - 2, NF)
    across = rem(f + 4, NF)
    twin = f + 1 - 2 * rem(f, 2)
    x_up, x_down = rem(x + 1, NX), rem(x + NX - 1, NX)

    barrier = pltpu.get_barrier_semaphore()

    @pl.loop(1, NS)
    def _(i):
        pl.semaphore_signal(barrier, 1, device_id={"se": rem(me + i, NS)}, device_id_type=MESH)

    for g in (up, down, across, twin):
        pl.semaphore_signal(barrier, 1, device_id={"freq": g}, device_id_type=MESH)

    small = [
        pltpu.make_async_copy(source, to, in_sem.at[k])
        for k, (source, to) in enumerate(
            ((t_hbm, t_ref), (sup_hbm, sup), (off_hbm, off), (cnt_hbm, cnt), (psd_hbm, psd_ref))
        )
    ]
    for copy in small:
        copy.start()
    tiles = table.shape[0]

    @pl.loop(0, tiles)
    def _(t):
        part = table_hbm.at[:, pl.ds(pl.multiple_of(t * 128, 128), 128)]
        pltpu.make_async_copy(part, table.at[t], table_sem).start()

    tin[...] = jnp.zeros_like(tin)
    small[0].wait()
    tin[:, 0:SHARD, :] = t_ref[...]
    tbuf[x, z] = tin[...]
    send_buf[:, PADDED - 16 : PADDED, :] = jnp.zeros((NS, 16, 128), bf16)

    pl.semaphore_wait(barrier, NS - 1 + 4)

    def tz_at(d):
        return rem(z + NZ + d, NZ)

    def tz_copy(step, k):
        half = FREQ_DEV // 2
        if step == 0:
            source, d = tbuf.at[x, z], (1, -1, 2, -2)[k]
        else:
            source, d = (
                (tbuf.at[x, tz_at(-2)], 1),
                (tbuf.at[x, tz_at(2)], -1),
                (tbuf.at[x, tz_at(-2), 0:half], 2),
                (tbuf.at[x, tz_at(2), half:FREQ_DEV], -2),
            )[k]
        return pltpu.make_async_remote_copy(
            src_ref=source, dst_ref=source, send_sem=tz_send.at[step], recv_sem=tz_recv.at[step],
            device_id={"se": tz_at(d) * NX + x}, device_id_type=MESH,
        )

    def tz_start(step):
        for k in range(4):
            tz_copy(step, k).start()

    def tz_wait(semaphores, step):
        some = tbuf.at[0, 0 : 4 - step]
        pltpu.make_async_copy(some, some, semaphores.at[step]).wait()

    tz_start(0)

    lane = lax.broadcasted_iota(jnp.int32, (LOCAL, 128), 1)

    def window(start, place):
        tile = div(start, 128)
        inside = start - tile * 128
        a = table[tile].astype(f32)
        b = table[jnp.minimum(tile + 1, tiles - 1)].astype(f32)
        both = jnp.where(lane >= inside, a, b)
        return pltpu.roll(both, rem(place + 128 - inside, 128), 1)

    def gather(o):
        base = o * PAN_DEV
        first, last = jnp.int32(0), jnp.int32(0)
        hits = [sup[base + j] == me for j in range(PAN_DEV)]
        starts = [off[base + j] for j in range(PAN_DEV)]
        for j in range(PAN_DEV):
            last = jnp.where(hits[j], starts[j], last)
            k = PAN_DEV - 1 - j
            first = jnp.where(hits[k], starts[k], first)
        got = jnp.where(lane < PROW, window(first, 0), window(last, PROW)).astype(bf16)
        send_buf[o, 0:LOCAL, :] = got

    def a2a_copy(c, o):
        r0, rows = CHUNKS[c]
        return pltpu.make_async_remote_copy(
            src_ref=send_buf.at[o, pl.ds(r0, rows)], dst_ref=rbs[c].at[me],
            send_sem=a2a_send.at[c], recv_sem=a2a_recv.at[c],
            device_id={"se": o}, device_id_type=MESH,
        )

    def a2a_start(c):
        @pl.loop(1, NS)
        def _(i):
            a2a_copy(c, rem(me + i, NS)).start()

    def a2a_sent(c):
        sent = rbs[c].at[0 : NS - 1]
        pltpu.make_async_copy(sent, sent, a2a_send.at[c]).wait()

    small[1].wait()
    small[2].wait()
    pltpu.make_async_copy(table, table, table_sem).wait()
    @pl.loop(0, NS, unroll=4)
    def _(o):
        gather(o)

    tz_wait(tz_recv, 0)
    tz_start(1)
    for c in range(len(CHUNKS)):
        a2a_start(c)
    for c, (r0, rows) in enumerate(CHUNKS):
        rbs[c][me] = send_buf[me, r0 : r0 + rows, :]

    def tx_copy(k):
        half = NZ // 2
        source, to = (
            (tbuf.at[x, 0:half], x_up),
            (tbuf.at[x, half:NZ], x_down),
            (tbuf.at[x, half:NZ], x_up),
            (tbuf.at[x, 0:half], x_down),
            (tbuf.at[x_down, 0:half], x_up),
            (tbuf.at[x_up, half:NZ], x_down),
        )[k]
        return pltpu.make_async_remote_copy(
            src_ref=source, dst_ref=source, send_sem=tx_send.at[k], recv_sem=tx_recv.at[k],
            device_id={"se": z * NX + to}, device_id_type=MESH,
        )

    tz_wait(tz_recv, 1)
    for k in range(4):
        tx_copy(k).start()

    small[3].wait()
    small[4].wait()
    half_lane = lax.broadcasted_iota(jnp.int32, (NI, 128), 1)
    i = lax.broadcasted_iota(jnp.int32, (128, 128), 0)
    j = lax.broadcasted_iota(jnp.int32, (128, 128), 1)
    swap = jnp.where(j == i + NI, 1.0, jnp.where(i == j + NI, -1.0, 0.0)).astype(bf16)
    for g in range(FREQ_DEV):
        turned = pltpu.roll(psd_ref[g].astype(f32), NI, 1)
        blocks_ref[g, 0:NI, 0:128] = psd_ref[g]
        blocks_ref[g, NI:128, 0:128] = jnp.where(half_lane < NI, -turned, turned).astype(bf16)
        blocks_ref[g, :, 128:256] = swap

    mine = me * PAN_DEV
    own = [sup[mine + p] for p in range(PAN_DEV)]
    for p in range(PAN_DEV):
        rank = jnp.int32(0)
        for e in range(p):
            rank = jnp.where(own[e] == own[p], 1, rank)
        ranks[p] = rank

    def rows_at(c, slot):
        rows = CHUNKS[c][1]
        return pl.ds(pl.multiple_of(PLACES[c][1] + slot * rows, 16), rows)

    def select(c):
        rows = CHUNKS[c][1]
        all_c = rbs[c].at[0 : NS - 1]
        pltpu.make_async_copy(all_c, all_c, a2a_recv.at[c]).wait()
        at = lax.broadcasted_iota(jnp.int32, (rows, 128), 1)

        @pl.loop(0, PAN_DEV // 2, unroll=4)
        def _(q):
            p = 2 * q
            left = rbs[c][sup[mine + p]].astype(f32)
            right = rbs[c][sup[mine + p + 1]].astype(f32)
            left = pltpu.roll(left, PROW * ranks[p], 1)
            right = pltpu.roll(right, PROW * (1 - ranks[p + 1]), 1)
            live = jnp.where(at < PROW, cnt[mine + p], cnt[mine + p + 1] + PROW)
            pair = jnp.where(at < live, jnp.where(at < PROW, left, right), 0.0)
            xgs[PLACES[c][0]][rows_at(c, f), pl.ds(pl.multiple_of(q * 128, 128), 128)] = pair.astype(bf16)

    def y_copy(c, k):
        slot, to = ((f, up), (f, down), (f, across), (f, twin), (down, twin), (up, twin), (across, twin))[k]
        source = xgs[PLACES[c][0]].at[rows_at(c, slot)]
        return pltpu.make_async_remote_copy(
            src_ref=source, dst_ref=source, send_sem=y_send.at[c, k], recv_sem=y_recv.at[c, k],
            device_id={"freq": to}, device_id_type=MESH,
        )

    def y_begin(c):
        for k in range(4):
            y_copy(c, k).start()

    def y_relay(c):
        for k in range(3):
            y_copy(c, k).wait_recv()
            y_copy(c, k + 4).start()

    def y_end(c):
        for k in range(3, 7):
            y_copy(c, k).wait_recv()

    def tx_forward():
        for k in (0, 1):
            tx_copy(k).wait_recv()
            tx_copy(k + 4).start()

    def tx_end():
        for k in (2, 3, 4, 5):
            tx_copy(k).wait_recv()

    def compact():
        k = lax.broadcasted_iota(jnp.int32, (PADDED, 128), 0)
        at = lax.broadcasted_iota(jnp.int32, (PADDED, 128), 1)
        mode = jnp.where(rem(at, TSH) < SHARD, div(at, TSH) * SHARD + rem(at, TSH), -1)
        pick = jnp.where(k == mode, 1.0, 0.0).astype(bf16)

        @pl.loop(0, NZ, unroll=2)
        def _(zz):
            blocks = [tbuf[:, zz, g].reshape(NX * TSH, 128) for g in range(FREQ_DEV)]
            rows_of = jnp.dot(pick, jnp.concatenate(blocks, axis=1), preferred_element_type=f32).astype(bf16)
            for c, (r0, rows) in enumerate(CHUNKS):
                tgs[PLACES[c][0]][rows_at(c, zz), :] = rows_of[r0 : r0 + rows]

    def multiply(group):
        step = 512

        @pl.loop(0, LANES // step)
        def _(n):
            at = pl.ds(pl.multiple_of(n * step, step), step)
            part = lax.dot_general(
                xgs[group][:, at], tgs[group][...], (((0,), (0,)), ((), ())), preferred_element_type=f32
            )
            if group == 0:
                acc[at, :] = part
            else:
                resp_ref[at, :] = (acc[at, :] + part).astype(bf16)

    select(0)
    y_begin(0)
    tx_forward()
    select(1)
    y_begin(1)
    y_relay(0)
    select(2)
    y_begin(2)
    y_relay(1)
    select(3)
    y_begin(3)
    tx_end()
    compact()
    y_end(0)
    y_end(1)
    multiply(0)
    y_relay(2)
    y_relay(3)
    y_end(2)
    y_end(3)
    multiply(1)

    tz_wait(tz_send, 0)
    tz_wait(tz_send, 1)
    for c in range(len(CHUNKS)):
        a2a_sent(c)
    for k in range(6):
        tx_copy(k).wait_send()
    for c in range(len(CHUNKS)):
        for k in range(7):
            y_copy(c, k).wait_send()


def responses(sup, off, cnt, table, transfer, psd):
    return pl.pallas_call(
        response_kernel,
        out_shape=[
            jax.ShapeDtypeStruct((LANES, WIDE), bf16),
            jax.ShapeDtypeStruct((FREQ_DEV, 128, 256), bf16),
        ],
        in_specs=[pl.BlockSpec(memory_space=pltpu.HBM)] * 6,
        out_specs=[pl.BlockSpec(memory_space=pltpu.VMEM)] * 2,
        scratch_shapes=[
            *[pltpu.SMEM(a.shape, jnp.int32) for a in (sup, off, cnt)],
            pltpu.VMEM(transfer.shape, bf16),
            pltpu.VMEM(psd.shape, bf16),
            pltpu.SemaphoreType.DMA((5,)),
            pltpu.VMEM((table.shape[1] // 128, LOCAL, 128), bf16),
            pltpu.VMEM((NS, PADDED, 128), bf16),
            *[pltpu.VMEM((NS, rows, 128), bf16) for _, rows in CHUNKS],
            *[pltpu.VMEM((deep, LANES), bf16) for deep in DEEP],
            *[pltpu.VMEM((deep, WIDE), bf16) for deep in DEEP],
            pltpu.VMEM((NX, NZ, FREQ_DEV, TSH, 128), bf16),
            pltpu.VMEM((FREQ_DEV, TSH, 128), bf16),
            pltpu.VMEM((LANES, WIDE), f32),
            pltpu.SMEM((PAN_DEV,), jnp.int32),
            pltpu.SemaphoreType.DMA,
            pltpu.SemaphoreType.DMA((len(CHUNKS),)),
            pltpu.SemaphoreType.DMA((len(CHUNKS),)),
            pltpu.SemaphoreType.DMA((len(CHUNKS), 7)),
            pltpu.SemaphoreType.DMA((len(CHUNKS), 7)),
            pltpu.SemaphoreType.DMA((2,)),
            pltpu.SemaphoreType.DMA((2,)),
            pltpu.SemaphoreType.DMA((6,)),
            pltpu.SemaphoreType.DMA((6,)),
        ],
        compiler_params=pltpu.CompilerParams(
            collective_id=0, has_side_effects=True, vmem_limit_bytes=44 * 2**20
        ),
        name="responses",
    )(*[pltpu.with_memory_space_constraint(a, pltpu.HBM) for a in (sup, off, cnt, table, transfer, psd)])


def spectra_kernel(resp_ref, blocks_ref, out_ref):
    for g in range(FREQ_DEV):
        resp = resp_ref[:, g * 128 : (g + 1) * 128]
        both = jnp.dot(resp, blocks_ref[g], preferred_element_type=f32).astype(bf16)
        for h in range(0, out_ref.shape[0], 2):
            one = slice(h * PROW, (h + 1) * PROW)
            two = slice((h + 1) * PROW, (h + 2) * PROW)
            pair = slice(h * PROW, (h + 2) * PROW)
            other = jnp.concatenate([resp[one], both[one, 128:256], resp[two], both[two, 128:256]], axis=0)
            cross = lax.dot_general(
                both[pair, 0:128], other, (((1,), (1,)), ((), ())), preferred_element_type=f32
            )
            out_ref[h, g] = cross[0:PROW, 0:128].astype(bf16)
            out_ref[h + 1, g] = cross[PROW:, 128:256].astype(bf16)


def spectra(resp, blocks):
    step = 1024
    return pl.pallas_call(
        spectra_kernel,
        grid=(LANES // step,),
        out_shape=jax.ShapeDtypeStruct((PAN_DEV, FREQ_DEV, PROW, 2 * NI), bf16),
        in_specs=[
            pl.BlockSpec((step, WIDE), lambda i: (i, 0)),
            pl.BlockSpec((FREQ_DEV, 128, 256), lambda i: (0, 0, 0)),
        ],
        out_specs=pl.BlockSpec((step // PROW, FREQ_DEV, PROW, 2 * NI), lambda i: (i, 0, 0, 0)),
        compiler_params=pltpu.CompilerParams(vmem_limit_bytes=16 * 2**20),
        name="spectra",
    )(resp, blocks)


def per_device(stress_modes, modal_transfer, input_psd, panel_super, panel_offset, panel_count):
    resp, blocks = responses(
        panel_super.reshape(-1), panel_offset, panel_count,
        stress_modes.T, modal_transfer.transpose(1, 0, 2), input_psd,
    )
    return spectra(resp, blocks)


def solution(mesh):
    in_specs = (P("se", "freq"), P("se", "freq", None), P("freq", None, None), P(), P(), P())
    out_specs = P("se", "freq", None, None)
    return jax.shard_map(
        per_device, mesh=mesh, in_specs=in_specs, out_specs=out_specs, check_vma=False
    )
```
